32 devices in a mesh: gene: 8 (over y, x, core), cell: 4 (over z).
Axes of the slice: x: 2, y: 2, z: 4, core: 2. Of those that a mesh axis runs over, the one named last changes fastest.
Arguments:
- counts: int32 [8192, 20000], P('cell', 'gene'), may hold values from 0 to 16, as said below
- labels: int32 [8192], P(('cell', 'gene')), may hold values from 0 to 127
- noise_draw: float32 [8192, 10], P(('cell', 'gene')), may hold values from -6 to 6
- enc_weight: float32 [20000, 128], P('gene'), may hold values from -0.0390625 to 0.0390625
- enc_first: float32 [20000, 128], P('gene'), may hold values from -0.00015258789 to 0.00015258789
- enc_second: float32 [20000, 128], P('gene'), may hold values from 8.053339e-12 to 3.2213357e-11
- out_weight: float32 [2, 128, 20000], P(None, None, 'gene'), may hold values from -0.5 to 0.5
- out_first: float32 [2, 128, 20000], P(None, None, 'gene'), may hold values from -0.00015258789 to 0.00015258789
- out_second: float32 [2, 128, 20000], P(None, None, 'gene'), may hold values from 8.053339e-12 to 3.2213357e-11
- gene_param: float32 [3, 20000], P(None, 'gene'), may hold values from -1 to 1
- gene_first: float32 [3, 20000], P(None, 'gene'), may hold values from -0.00015258789 to 0.00015258789
- gene_second: float32 [3, 20000], P(None, 'gene'), may hold values from 8.053339e-12 to 3.2213357e-11
- head_weight: float32 [128, 20], replicated, may hold values from -0.5 to 0.5
- head_first: float32 [128, 20], replicated, may hold values from -0.00015258789 to 0.00015258789
- head_second: float32 [128, 20], replicated, may hold values from 8.053339e-12 to 3.2213357e-11
- head_bias: float32 [20], replicated, may hold values from -4 to 4
- bias_first: float32 [20], replicated, may hold values from -0.00015258789 to 0.00015258789
- bias_second: float32 [20], replicated, may hold values from 8.053339e-12 to 3.2213357e-11
- dec_weight: float32 [138, 128], replicated, may hold values from -0.5 to 0.5
- dec_first: float32 [138, 128], replicated, may hold values from -0.00015258789 to 0.00015258789
- dec_second: float32 [138, 128], replicated, may hold values from 8.053339e-12 to 3.2213357e-11
- norm_param: float32 [4, 128], replicated, may hold values from 0.5 to 1.5
- norm_first: float32 [4, 128], replicated, may hold values from -0.00015258789 to 0.00015258789
- norm_second: float32 [4, 128], replicated, may hold values from 8.053339e-12 to 3.2213357e-11
Outputs:
- loss_sum: float32 [], replicated
- grad_norm: float32 [], replicated
- enc_master: float32 [20000, 128], P('gene')
- enc_first_new: float32 [20000, 128], P('gene')
- enc_second_new: float32 [20000, 128], P('gene')
- out_master: float32 [2, 128, 20000], P(None, None, 'gene')
- out_first_new: float32 [2, 128, 20000], P(None, None, 'gene')
- out_second_new: float32 [2, 128, 20000], P(None, None, 'gene')
- gene_master: float32 [3, 20000], P(None, 'gene')
- gene_first_new: float32 [3, 20000], P(None, 'gene')
- gene_second_new: float32 [3, 20000], P(None, 'gene')
- head_master: float32 [128, 20], replicated
- head_first_new: float32 [128, 20], replicated
- head_second_new: float32 [128, 20], replicated
- bias_master: float32 [20], replicated
- bias_first_new: float32 [20], replicated
- bias_second_new: float32 [20], replicated
- dec_master: float32 [138, 128], replicated
- dec_first_new: float32 [138, 128], replicated
- dec_second_new: float32 [138, 128], replicated
- norm_master: float32 [4, 128], replicated
- norm_first_new: float32 [4, 128], replicated
- norm_second_new: float32 [4, 128], replicated
- enc_copy: bfloat16 [20000, 128], P('gene')
- out_copy: bfloat16 [2, 128, 20000], P(None, None, 'gene')
- head_copy: bfloat16 [128, 20], replicated
- dec_copy: bfloat16 [138, 128], replicated
The draws below stay inside these ranges and needn't reach their ends.
Inputs may be any that keep to these rules, and one draw needn't show every extreme that they name: `counts`: every cell has a count of 1 or more in some gene.
All inputs are finite; a program needn't handle non-finite values.
Results may differ from the reference program's by a relative error of at most 0.0095.
Values may be sent and summed in bfloat16 or wider, within the bound.
No kernel may reach another device: no remote copies, remote signals or barrier semaphores. Data moves between devices by JAX's collectives and lax.ppermute only.
A program may use at most 256 MiB of HBM per device.

```python
import math
import jax
import jax.numpy as jnp
from jax import lax

H = 128
L = 10
G = 20000
NB = 128
STEP = 10
CELLS = 8192
NPARAM = 7760756
N_CELL = 4


def draw_counts(key, part):
    key = jax.random.fold_in(key, 1)
    keys = jax.random.split(key, 6)
    rows = jnp.arange(CELLS)
    depth = 1 + jax.random.randint(keys[0], (CELLS,), 0, 3) + 6 * rows // CELLS
    genes = jnp.arange(G)
    present = jax.random.randint(keys[1], (CELLS, G), 0, 8 * G) < (G + 2 * genes)[None, :]
    values = jax.random.randint(keys[2], (CELLS, G), 0, 2 * depth[:, None] + 1)
    counts = jnp.where(present, values, 0)
    picked = jax.random.randint(keys[3], (CELLS,), 0, G)
    counts = counts.at[rows, picked].set(jnp.maximum(counts[rows, picked], 1))
    row_top = jax.random.randint(keys[4], (), 0, CELLS)
    gene_top = jax.random.randint(keys[5], (), 0, G)
    counts = counts.at[row_top, gene_top].set(16)
    return counts.astype(jnp.int32)


def touch_ends(array, rng, low, top_value):
    dims = array.shape
    spot = [jax.random.randint(jax.random.fold_in(rng, axis), (), 0, dims[axis]) for axis in range(len(dims))]
    array = array.at[tuple(spot)].set(low)
    longest = dims.index(max(dims))
    spot[longest] = (spot[longest] + 1) % dims[longest]
    return array.at[tuple(spot)].set(top_value)


def block_levels(stream_key, shape, cuts, low, top_value):
    level = 1.0
    for dim, shards_of in cuts:
        heights = jax.random.uniform(jax.random.fold_in(jax.random.fold_in(stream_key, 6), dim), (shards_of,), jnp.float32, low / len(cuts), top_value / len(cuts))
        level = level * jnp.repeat(jnp.exp(heights), shape[dim] // shards_of).reshape((-1,) + (1,) * (len(shape) - 1 - dim))
    return level


def gaussian(key, dims, width, most, cuts=(), kind=jnp.bfloat16):
    level = block_levels(key, dims, cuts, -0.22, 0.18) if cuts else 1.0
    values = jax.random.normal(key, dims, jnp.float32) * width * level
    return jnp.minimum(jnp.maximum(values, -most), most).astype(kind)


def setup_inputs(seed: int = 0) -> dict:
    key_list = jax.random.split(jax.random.key(seed), 25)
    counts = draw_counts(jax.random.fold_in(key_list[24], 71), 0)
    labels = touch_ends(jax.random.randint(key_list[1], (CELLS,), 0, NB), jax.random.fold_in(key_list[1], 1), 0, NB - 1).astype(jnp.int32)
    noise_draw = gaussian(key_list[2], (CELLS, L), 1.0, 6.0, ((0, 32),), jnp.float32)
    enc_weight = gaussian(key_list[3], (G, H), G ** -0.5, 0.0390625, ((0, 8),), jnp.float32)
    enc_first = gaussian(key_list[4], (G, H), (0.028 / NPARAM ** 0.5), 0.00015258789, ((0, 8),), jnp.float32)
    enc_second = jnp.clip(jnp.exp(math.log(3.221335698189165e-11) - 1.3862944 * jax.random.uniform(key_list[5], (G, H), jnp.float32) ** block_levels(key_list[5], (G, H), ((0, 8),), -0.2, 0.2)), 8.053339245472912e-12, 3.221335698189165e-11)
    out_weight = gaussian(key_list[6], (2, H, G), H ** -0.5, 0.5, ((2, 8),), jnp.float32)
    out_first = gaussian(key_list[7], (2, H, G), (0.028 / NPARAM ** 0.5), 0.00015258789, ((2, 8),), jnp.float32)
    out_second = jnp.clip(jnp.exp(math.log(3.221335698189165e-11) - 1.3862944 * jax.random.uniform(key_list[8], (2, H, G), jnp.float32) ** block_levels(key_list[8], (2, H, G), ((2, 8),), -0.2, 0.2)), 8.053339245472912e-12, 3.221335698189165e-11)
    gene_param = jnp.clip(jax.random.uniform(key_list[9], (3, G), jnp.float32, -1.0, 1.0) * block_levels(key_list[9], (3, G), ((1, 8),), -0.4, 0.0), -1.0, 1.0)
    gene_first = gaussian(key_list[10], (3, G), (0.028 / NPARAM ** 0.5), 0.00015258789, ((1, 8),), jnp.float32)
    gene_second = jnp.clip(jnp.exp(math.log(3.221335698189165e-11) - 1.3862944 * jax.random.uniform(key_list[11], (3, G), jnp.float32) ** block_levels(key_list[11], (3, G), ((1, 8),), -0.2, 0.2)), 8.053339245472912e-12, 3.221335698189165e-11)
    head_weight = gaussian(key_list[12], (H, 2 * L), H ** -0.5, 0.5, (), jnp.float32)
    head_first = gaussian(key_list[13], (H, 2 * L), (0.028 / NPARAM ** 0.5), 0.00015258789, (), jnp.float32)
    head_second = jnp.clip(jnp.exp(jax.random.uniform(key_list[14], (H, 2 * L), jnp.float32, math.log(8.053339245472912e-12), math.log(3.221335698189165e-11))), 8.053339245472912e-12, 3.221335698189165e-11)
    head_bias = gaussian(key_list[15], (2 * L,), 0.3, 4.0, (), jnp.float32)
    bias_first = gaussian(key_list[16], (2 * L,), (0.028 / NPARAM ** 0.5), 0.00015258789, (), jnp.float32)
    bias_second = jnp.clip(jnp.exp(jax.random.uniform(key_list[17], (2 * L,), jnp.float32, math.log(8.053339245472912e-12), math.log(3.221335698189165e-11))), 8.053339245472912e-12, 3.221335698189165e-11)
    dec_weight = gaussian(key_list[18], (L + NB, H), (L + NB) ** -0.5, 0.5, (), jnp.float32)
    dec_first = gaussian(key_list[19], (L + NB, H), (0.028 / NPARAM ** 0.5), 0.00015258789, (), jnp.float32)
    dec_second = jnp.clip(jnp.exp(jax.random.uniform(key_list[20], (L + NB, H), jnp.float32, math.log(8.053339245472912e-12), math.log(3.221335698189165e-11))), 8.053339245472912e-12, 3.221335698189165e-11)
    norm_param = jnp.clip(1.0 + 0.1 * jax.random.normal(key_list[21], (4, H), jnp.float32), 0.5, 1.5)
    norm_first = gaussian(key_list[22], (4, H), (0.028 / NPARAM ** 0.5), 0.00015258789, (), jnp.float32)
    norm_second = jnp.clip(jnp.exp(jax.random.uniform(key_list[23], (4, H), jnp.float32, math.log(8.053339245472912e-12), math.log(3.221335698189165e-11))), 8.053339245472912e-12, 3.221335698189165e-11)
    return {"counts": counts, "labels": labels, "noise_draw": noise_draw, "enc_weight": enc_weight, "enc_first": enc_first, "enc_second": enc_second, "out_weight": out_weight, "out_first": out_first, "out_second": out_second, "gene_param": gene_param, "gene_first": gene_first, "gene_second": gene_second, "head_weight": head_weight, "head_first": head_first, "head_second": head_second, "head_bias": head_bias, "bias_first": bias_first, "bias_second": bias_second, "dec_weight": dec_weight, "dec_first": dec_first, "dec_second": dec_second, "norm_param": norm_param, "norm_first": norm_first, "norm_second": norm_second}


HIGHEST = lax.Precision.HIGHEST
BETA_ONE = 0.9
BETA_TWO = 0.999
ADAM_EPS = 1e-08
DECAY_RATE = 0.01
CLIP_NORM = 0.25
NORM_EPS = 0.001

@jax.custom_vjp
def low(v):
    return lax.optimization_barrier(v.astype(jnp.bfloat16)).astype(jnp.float32)

@jax.custom_vjp
def low_back(v):
    return v

def low_keep(v):
    return (low(v), None)

def low_pass(kept, grad):
    return (grad,)

def back_keep(v):
    return (v, None)

def back_low(kept, grad):
    return (low(grad),)
low.defvjp(low_keep, low_pass)
low_back.defvjp(back_keep, back_low)

def sigmoid_unit(value):
    return value * jax.nn.sigmoid(value)

def batch_norm(hidden, gain, shift):
    average = lax.optimization_barrier(jnp.mean(hidden, 0))
    variance = lax.optimization_barrier(jnp.mean(hidden * hidden, 0)) - average * average
    return (hidden - average) * lax.rsqrt(variance + NORM_EPS) * gain + shift

def zinb_terms(counts, log_mean, dropout, log_theta):
    theta = jnp.exp(log_theta)
    log_both = jnp.logaddexp(log_theta, log_mean)
    soft_neg = jax.nn.softplus(-dropout)
    shifted = -dropout + theta * (log_theta - log_both)
    zero_case = jax.nn.softplus(shifted) - soft_neg
    fcounts = counts.astype(jnp.float32)
    theta_full = jnp.broadcast_to(theta, fcounts.shape)
    other_case = -soft_neg + shifted + fcounts * (log_mean - log_both) + lax.lgamma(fcounts + theta_full) - lax.lgamma(theta_full) - lax.lgamma(fcounts + 1.0)
    return jnp.where(counts == 0, zero_case, other_case)

def forward(enc_w, out_w, gene_p, head_w, head_b, dec_w, norm_p, counts, labels, noise_draw):
    ncells = counts.shape[0]
    blocks = counts.reshape(N_CELL, ncells // N_CELL, G)
    enc_low = low(enc_w)

    def enc_block(block):
        return jnp.dot(low(jnp.log1p(block.astype(jnp.float32))), enc_low, precision=HIGHEST)
    enc_hidden = low_back(lax.map(jax.checkpoint(enc_block), blocks).reshape(ncells, H))
    enc_out = low(sigmoid_unit(batch_norm(enc_hidden, norm_p[0], norm_p[1])))
    head_out = jnp.dot(enc_out, low(head_w), precision=HIGHEST) + head_b
    latent_mean = head_out[:, :L]
    log_var = head_out[:, L:]
    latent = latent_mean + jnp.exp(0.5 * log_var) * noise_draw
    kl_sum = 0.5 * jnp.sum(latent_mean * latent_mean + jnp.exp(log_var) - log_var - 1.0)
    onehot = (labels[:, None] == jnp.arange(NB)[None, :]).astype(jnp.float32)
    dec_in = jnp.concatenate([low(latent), onehot], 1)
    pre_two = jnp.dot(dec_in, low(dec_w), precision=HIGHEST)
    dec_hidden = low(sigmoid_unit(batch_norm(pre_two, norm_p[2], norm_p[3])))
    out_low = low(out_w)

    def dec_block(pair):
        hidden_rows, count_rows = pair
        logits = low_back(jnp.dot(hidden_rows, out_low[0], precision=HIGHEST) + gene_p[0])
        dropout = low_back(jnp.dot(hidden_rows, out_low[1], precision=HIGHEST) + gene_p[1])
        log_scale = logits - jax.nn.logsumexp(logits, axis=1, keepdims=True)
        log_total = jnp.log(lax.optimization_barrier(jnp.sum(count_rows.astype(jnp.float32), 1, keepdims=True)))
        return -jnp.sum(zinb_terms(count_rows, log_total + log_scale, dropout, gene_p[2]))
    recon = jnp.sum(lax.map(jax.checkpoint(dec_block), (dec_hidden.reshape(N_CELL, -1, H), blocks)))
    total = recon + kl_sum
    return (total / ncells, total)

def adam_update(master, first, second, grad, rate):
    first_new = BETA_ONE * first + (1.0 - BETA_ONE) * grad
    second_new = BETA_TWO * second + (1.0 - BETA_TWO) * grad * grad
    first_hat = first_new / (1.0 - BETA_ONE ** STEP)
    second_hat = second_new / (1.0 - BETA_TWO ** STEP)
    master_new = master - rate * (first_hat / (jnp.sqrt(second_hat) + ADAM_EPS) + DECAY_RATE * master)
    return (master_new, first_new, second_new)

def reference(counts, labels, noise_draw, enc_weight, enc_first, enc_second, out_weight, out_first, out_second, gene_param, gene_first, gene_second, head_weight, head_first, head_second, head_bias, bias_first, bias_second, dec_weight, dec_first, dec_second, norm_param, norm_first, norm_second):
    params = (enc_weight, out_weight, gene_param, head_weight, head_bias, dec_weight, norm_param)

    def objective(*weights):
        return forward(*weights, counts, labels, noise_draw)
    mean_loss, pull_back, loss_sum = jax.vjp(objective, *params, has_aux=True)
    grads = pull_back(jnp.ones_like(mean_loss))
    squares = grads[0][0, 0] * 0.0
    for grad in grads:
        squares = squares + jnp.sum(grad * grad)
    grad_norm = jnp.sqrt(squares)
    factor = jnp.minimum(1.0, CLIP_NORM / (grad_norm + 1e-06))
    rates = (G ** (-0.5), H ** (-0.5), 0.3, H ** (-0.5), 0.3, (L + NB) ** (-0.5), 0.3)
    firsts = (enc_first, out_first, gene_first, head_first, bias_first, dec_first, norm_first)
    seconds = (enc_second, out_second, gene_second, head_second, bias_second, dec_second, norm_second)
    results = []
    for index in range(7):
        results.append(adam_update(params[index], firsts[index], seconds[index], grads[index] * factor, rates[index]))
    return (loss_sum, grad_norm, results[0][0], results[0][1], results[0][2], results[1][0], results[1][1], results[1][2], results[2][0], results[2][1], results[2][2], results[3][0], results[3][1], results[3][2], results[4][0], results[4][1], results[4][2], results[5][0], results[5][1], results[5][2], results[6][0], results[6][1], results[6][2], results[0][0].astype(jnp.bfloat16), results[1][0].astype(jnp.bfloat16), results[3][0].astype(jnp.bfloat16), results[5][0].astype(jnp.bfloat16))
```

```python
import jax
import jax.numpy as jnp
from jax import lax
from jax.experimental import pallas as pl
from jax.experimental.pallas import tpu as pltpu
from jax.sharding import PartitionSpec as P

L = 10
NB = 128
STEP = 10
G = 20000
H = 128
BETA_ONE = 0.9
BETA_TWO = 0.999
ADAM_EPS = 1e-08
DECAY_RATE = 0.01
CLIP_NORM = 0.25
NORM_EPS = 0.001
TOP_COUNT = 16
LOG2E = 1.4426950408889634
LN2 = 0.6931471805599453
DROP_TOP = 60.0
FAR_DOWN = -1e30
KA = 144
CELL_BLOCK = 256
LANE_BLOCK = 512
F32 = jnp.float32
BF16 = jnp.bfloat16
VMEM_BYTES = 56 * 2**20


def round_up(value, unit):
    return -(-value // unit) * unit


def gene_tile(padded):
    return 256 if padded % 256 == 0 else 128


def turned_block(block, devices, per_device_blocks):
    owner = block // per_device_blocks
    out = 0
    bit = 1
    while bit < devices:
        out = 2 * out + (owner // bit) % 2
        bit *= 2
    return out * per_device_blocks + block % per_device_blocks


def params(flops=0, read=0):
    return dict(
        compiler_params=pltpu.CompilerParams(vmem_limit_bytes=VMEM_BYTES),
        cost_estimate=pl.CostEstimate(flops=flops, bytes_accessed=read, transcendentals=0),
    )


def dot(left, right):
    return jnp.dot(left, right, preferred_element_type=F32)


def dot_nt(left, right):
    return lax.dot_general(left, right, (((1,), (1,)), ((), ())), preferred_element_type=F32)


def dot_tn(left, right):
    return lax.dot_general(left, right, (((0,), (0,)), ((), ())), preferred_element_type=F32)


def two_parts(value):
    high = value.astype(BF16)
    return high, (value - high.astype(F32)).astype(BF16)


def as_column(row, lanes):
    square = jnp.transpose(jnp.broadcast_to(row, (128, 128)))
    return jnp.concatenate([square] * (lanes // 128), axis=1)


def lane_sums_row(value):
    total = value[:, :128]
    for k in range(1, value.shape[1] // 128):
        total = total + value[:, k * 128 : (k + 1) * 128]
    return jnp.sum(jnp.transpose(total), axis=0, keepdims=True)


def stack_rows(rows):
    wide = rows[0].shape[1]
    index = lax.broadcasted_iota(jnp.int32, (8, wide), 0)
    out = jnp.zeros((8, wide), F32)
    for k, row in enumerate(rows):
        out = jnp.where(index == k, jnp.broadcast_to(row, (8, wide)), out)
    return out


def sigmoid(value):
    return 1.0 / (1.0 + jnp.exp(-value))


def log_counts(block, first_row, genes):
    if first_row + block.shape[0] > genes:
        row = lax.broadcasted_iota(jnp.int32, block.shape, 0) + first_row
        block = jnp.where(row < genes, block, 0)
    value = block.astype(F32)
    return value, (jnp.log2(value + 1.0) * LN2).astype(BF16)


def encoder_sums(counts, enc_weight, place):
    genes, cells = counts.shape
    padded = round_up(genes, 128)
    tile = gene_tile(padded)
    tc = CELL_BLOCK

    def kernel(cnt_ref, w_ref, out_ref, tot_ref, wlow, xs):
        @pl.when(pl.program_id(0) == 0)
        def _():
            for k in range(padded // 128):
                rows = lax.broadcasted_iota(jnp.int32, (128, 128), 0) + k * 128
                part = jnp.where(rows < genes, w_ref[k * 128 : (k + 1) * 128, :], 0.0)
                wlow[:, k * 128 : (k + 1) * 128] = jnp.transpose(part).astype(BF16)

        total = jnp.zeros((8, tc), F32)
        out = jnp.zeros((128, tc), F32)
        for j in range(padded // tile):
            for r in range(0, tile, 16):
                at = slice(j * tile + r, j * tile + r + 16)
                value, low = log_counts(cnt_ref[at, :], j * tile + r, genes)
                xs[at, :] = low
                total = total + (value[0:8] + value[8:16])
            span = slice(j * tile, (j + 1) * tile)
            out = out + dot(wlow[:, span], xs[span, :])
        out_ref[...] = out
        tot_ref[...] = jnp.broadcast_to(jnp.sum(total, axis=0, keepdims=True), (8, tc))

    return pl.pallas_call(
        kernel,
        grid=(cells // tc,),
        in_specs=[
            pl.BlockSpec((padded, tc), lambda i: (0, i)),
            pl.BlockSpec((padded, 128), lambda i: (0, 0)),
        ],
        out_specs=[
            pl.BlockSpec((128, tc), lambda i: (0, place(i))),
            pl.BlockSpec((8, tc), lambda i: (0, place(i))),
        ],
        out_shape=[
            jax.ShapeDtypeStruct((128, cells), F32),
            jax.ShapeDtypeStruct((8, cells), F32),
        ],
        scratch_shapes=[
            pltpu.VMEM((128, padded), BF16),
            pltpu.VMEM((padded, tc), BF16),
        ],
        name="encoder_sums",
        **params(2 * cells * padded * 128, 4 * cells * padded),
    )(counts, enc_weight)


def three_parts(value):
    high = value.astype(BF16).astype(F32)
    middle = (value - high).astype(BF16).astype(F32)
    return high, middle, value - high - middle


def decoder_weights(out_rows, gene_param):
    genes = gene_param.shape[1]
    padded = round_up(genes, 128)
    tile = gene_tile(padded)

    def kernel(
        w_ref, gene_ref, wy_ref, wd_ref, zero_ref, one_ref, mixed_ref, theta_ref, sum_ref, slope_ref
    ):
        first = pl.program_id(0) * tile
        row = lax.broadcasted_iota(jnp.int32, (tile, 128), 0) + first
        lane = lax.broadcasted_iota(jnp.int32, (tile, 128), 1)
        inside = row < genes
        zero = jnp.where(inside, w_ref[pl.ds(0, tile, stride=2), :], 0.0)
        one = jnp.where(inside, w_ref[pl.ds(1, tile, stride=2), :], 0.0)
        low_zero = zero.astype(BF16)
        turned = jnp.transpose(jnp.concatenate([gene_ref[...], jnp.zeros((125, tile), F32)], 0))

        def column(k, outside):
            wide = jnp.broadcast_to(turned[:, k : k + 1], (tile, 128))
            return jnp.where(inside, wide, outside)

        bias = column(0, FAR_DOWN)
        drop_bias = column(1, 0.0)
        log_theta = column(2, 0.0)
        theta = jnp.exp(log_theta)

        def pieces(value, at, out):
            for k, part in enumerate(three_parts(value)):
                out = jnp.where(lane == at + k, part, out)
            return out

        ones = jnp.where((lane >= 3) & (lane < 6), 1.0, 0.0)
        side = pieces(log_theta, 6, pieces(bias - log_theta, 0, ones))
        wy_ref[:, 0:128] = low_zero
        wy_ref[:, 128:256] = side.astype(BF16)
        wd_ref[:, 0:128] = one.astype(BF16)
        wd_ref[:, 128:256] = pieces(drop_bias, 0, jnp.zeros((tile, 128), F32)).astype(BF16)
        zero_ref[0:128, :] = jnp.transpose(zero).astype(BF16)
        one_ref[0:128, :] = jnp.transpose(one).astype(BF16)
        across = lax.broadcasted_iota(jnp.int32, (16, tile), 1) + first
        below = lax.broadcasted_iota(jnp.int32, (16, tile), 0)
        zero_ref[128:144, :] = jnp.where((across < genes) & (below == 0), 1.0, 0.0).astype(BF16)
        one_ref[128:144, :] = jnp.zeros((16, tile), BF16)
        mixed_ref[...] = jnp.transpose(low_zero.astype(F32) * theta).astype(BF16)
        theta_ref[...] = theta
        number = lane.astype(F32)
        known = lane < TOP_COUNT
        steps = jnp.where(known, jnp.log2((theta + number) / (number + 1.0)), 0.0)
        slopes = jnp.where(known, (1.0 / LN2) / (theta + number), 0.0)
        index = lax.broadcasted_iota(jnp.int32, (128, 128), 0)
        other = lax.broadcasted_iota(jnp.int32, (128, 128), 1)
        before = jnp.where(index < other, 1.0, 0.0).astype(BF16)

        def running(value):
            out = jnp.zeros((tile, 128), F32)
            for part in three_parts(value):
                out = out + dot(part.astype(BF16), before)
            return out

        sum_ref[...] = running(steps)
        slope_ref[...] = running(slopes)

    shape = jax.ShapeDtypeStruct
    down = lambda j: (j, 0)
    right = lambda j: (0, j)
    return pl.pallas_call(
        kernel,
        grid=(padded // tile,),
        in_specs=[pl.BlockSpec((2 * tile, 128), down), pl.BlockSpec((3, tile), right)],
        out_specs=[
            pl.BlockSpec((tile, 256), down),
            pl.BlockSpec((tile, 256), down),
            pl.BlockSpec((144, tile), right),
            pl.BlockSpec((144, tile), right),
            pl.BlockSpec((128, tile), right),
            pl.BlockSpec((tile, 128), down),
            pl.BlockSpec((tile, 128), down),
            pl.BlockSpec((tile, 128), down),
        ],
        out_shape=[
            shape((padded, 256), BF16),
            shape((padded, 256), BF16),
            shape((144, padded), BF16),
            shape((144, padded), BF16),
            shape((128, padded), BF16),
            shape((padded, 128), F32),
            shape((padded, 128), F32),
            shape((padded, 128), F32),
        ],
        name="decoder_weights",
        **params(100 * 128 * padded, 20 * 128 * padded),
    )(out_rows, gene_param)


def norm_rows(sums, gain, total):
    average = sums[0:1] * (1.0 / total)
    variance = sums[1:2] * (1.0 / total) - average * average
    return average, lax.rsqrt(variance + NORM_EPS)


def hidden_stats(hidden):
    cells = hidden.shape[1]
    block = min(cells, 1024)

    def kernel(h_ref, out_ref):
        one = jnp.zeros((128, 128), F32)
        two = jnp.zeros((128, 128), F32)
        for k in range(block // 128):
            value = h_ref[:, k * 128 : (k + 1) * 128].astype(F32)
            one = one + value
            two = two + value * value
        rows = stack_rows([lane_sums_row(one), lane_sums_row(two)])

        @pl.when(pl.program_id(0) == 0)
        def _():
            out_ref[...] = rows

        @pl.when(pl.program_id(0) > 0)
        def _():
            out_ref[...] += rows

    return pl.pallas_call(
        kernel,
        grid=(cells // block,),
        in_specs=[pl.BlockSpec((128, block), lambda i: (0, i))],
        out_specs=pl.BlockSpec((8, 128), lambda i: (0, 0)),
        out_shape=jax.ShapeDtypeStruct((8, 128), F32),
        name="hidden_stats",
        **params(4 * cells * 128, 2 * cells * 128),
    )(hidden)


def head_terms(h, sums, norm_ref, head_ref, bias_ref, noise, total, lanes):
    average, inv = norm_rows(sums, None, total)
    normed = (h.astype(F32) - as_column(average, lanes)) * as_column(inv, lanes)
    act = normed * as_column(norm_ref[0:1], lanes) + as_column(norm_ref[1:2], lanes)
    gate = sigmoid(act)
    enc_out = (act * gate).astype(BF16)
    head_out = dot(head_ref[...], enc_out) + bias_ref[:, 0:1]
    mean = head_out[0:16]
    log_var = head_out[16:32]
    spread = jnp.exp(0.5 * log_var)
    latent = mean + spread * noise
    return normed, act, gate, enc_out, mean, log_var, spread, latent


def unpack_extra(extra):
    noise = extra[0:16].astype(F32) + extra[16:32].astype(F32)
    label = noise[10:11]
    row = lax.broadcasted_iota(jnp.int32, noise.shape, 0)
    return jnp.where(row < L, noise, 0.0), label


def decoder_input(latent, label):
    index = lax.broadcasted_iota(jnp.int32, (128, label.shape[1]), 0).astype(F32)
    onehot = jnp.where(index == label, 1.0, 0.0).astype(BF16)
    return jnp.concatenate([latent.astype(BF16), onehot], axis=0)


def encoder_heads(gathered, sums, norm_param, head_low, head_bias, dec_low, total):
    cells = gathered.shape[1]
    block = min(cells, LANE_BLOCK)

    def kernel(g_ref, s_ref, norm_ref, head_ref, bias_ref, dec_ref, pre_ref, out_ref):
        noise, label = unpack_extra(g_ref[128:160, :])
        terms = head_terms(
            g_ref[0:128, :], s_ref[...], norm_ref, head_ref, bias_ref, noise, total, block
        )
        mean, log_var, latent = terms[4], terms[5], terms[7]
        pre = dot_tn(dec_ref[...], decoder_input(latent, label))
        pre_ref[...] = pre
        diverge = mean * mean + jnp.exp(log_var) - log_var - 1.0
        kl_row = diverge[0:8, 0:128] + diverge[8:16, 0:128]
        for k in range(1, block // 128):
            span = slice(k * 128, (k + 1) * 128)
            kl_row = kl_row + diverge[0:8, span] + diverge[8:16, span]
        kl_row = 0.5 * jnp.sum(kl_row, axis=0, keepdims=True)
        rows = stack_rows([lane_sums_row(pre), lane_sums_row(pre * pre), kl_row])

        @pl.when(pl.program_id(0) == 0)
        def _():
            out_ref[...] = rows

        @pl.when(pl.program_id(0) > 0)
        def _():
            out_ref[...] += rows

    whole = lambda i: (0, 0)
    return pl.pallas_call(
        kernel,
        grid=(cells // block,),
        in_specs=[
            pl.BlockSpec((160, block), lambda i: (0, i)),
            pl.BlockSpec((8, 128), whole),
            pl.BlockSpec((4, 128), whole),
            pl.BlockSpec((32, 128), whole),
            pl.BlockSpec((32, 128), whole),
            pl.BlockSpec((144, 128), whole),
        ],
        out_specs=[pl.BlockSpec((128, block), lambda i: (0, i)), pl.BlockSpec((8, 128), whole)],
        out_shape=[
            jax.ShapeDtypeStruct((128, cells), F32),
            jax.ShapeDtypeStruct((8, 128), F32),
        ],
        name="encoder_heads",
        **params(2 * cells * 128 * 180, 8 * cells * 128),
    )(gathered, sums, norm_param, head_low, head_bias, dec_low)


def decoder_scan(pre, sums, norm_param, tot_rows, wy, total, devices):
    cells = pre.shape[1]
    padded = wy.shape[0]
    tile = gene_tile(padded)
    tiles = padded // tile
    tc = 2 * CELL_BLOCK

    def kernel(pre_ref, s_ref, norm_ref, tot_ref, wy_ref, hid_ref, turned_ref, rows_ref, rhs, raw):
        average, inv = norm_rows(s_ref[...], None, total)
        scale = inv * norm_ref[2:3]
        offset = norm_ref[3:4] - average * scale
        act = pre_ref[...] * as_column(scale, tc) + as_column(offset, tc)
        hidden = act * sigmoid(act)
        low = hidden.astype(BF16)
        turned_ref[...] = low
        hid_ref[...] = jnp.transpose(hidden).astype(BF16)
        rhs[0:128, :] = low
        index = lax.broadcasted_iota(jnp.int32, (128, tc), 0)
        used = (index < 3) | ((index >= 6) & (index < 9))
        rhs[128:256, :] = jnp.where(used, 1.0, 0.0).astype(BF16)

        def logits(j):
            raw[j % 2] = dot(wy_ref[j * tile : (j + 1) * tile, :], rhs[...])

        logits(0)
        top = jnp.full((8, tc), 4.0 * FAR_DOWN, F32)
        exp_sum = jnp.zeros((8, tc), F32)
        for j in range(tiles):
            if j + 1 < tiles:
                logits(j + 1)
            best = top
            for r in range(0, tile, 8):
                best = jnp.maximum(best, raw[j % 2, r : r + 8, :])
            down = best * LOG2E
            exp_sum = exp_sum * jnp.exp2(top * LOG2E - down)
            for r in range(0, tile, 8):
                exp_sum = exp_sum + jnp.exp2(raw[j % 2, r : r + 8, :] * LOG2E - down)
            top = best
        highest = jnp.max(top, axis=0, keepdims=True)
        merged = jnp.sum(exp_sum * jnp.exp(top - highest), axis=0, keepdims=True)
        rows = stack_rows([highest + jnp.log(merged), tot_ref[0:1, :]])[0:2]
        for k in range(devices):
            rows_ref[k] = rows

    whole = lambda i: (0, 0)
    return pl.pallas_call(
        kernel,
        grid=(cells // tc,),
        in_specs=[
            pl.BlockSpec((128, tc), lambda i: (0, i)),
            pl.BlockSpec((8, 128), whole),
            pl.BlockSpec((4, 128), whole),
            pl.BlockSpec((8, tc), lambda i: (0, i)),
            pl.BlockSpec((padded, 256), whole),
        ],
        out_specs=[
            pl.BlockSpec((tc, 128), lambda i: (i, 0)),
            pl.BlockSpec((128, tc), lambda i: (0, i)),
            pl.BlockSpec((devices, 2, tc), lambda i: (0, 0, i)),
        ],
        out_shape=[
            jax.ShapeDtypeStruct((cells, 128), BF16),
            jax.ShapeDtypeStruct((128, cells), BF16),
            jax.ShapeDtypeStruct((devices, 2, cells), F32),
        ],
        scratch_shapes=[
            pltpu.VMEM((256, tc), BF16),
            pltpu.VMEM((2, tile, tc), F32),
        ],
        name="decoder_scan",
        **params(2 * cells * padded * 128, 4 * cells * 128),
    )(pre, sums, norm_param, tot_rows, wy)


def combine_rows(rows_ref):
    count = rows_ref.shape[0]
    top = rows_ref[0, 0:1, :]
    for k in range(1, count):
        top = jnp.maximum(top, rows_ref[k, 0:1, :])
    exp_sum = jnp.zeros_like(top)
    total = jnp.zeros_like(top)
    for k in range(count):
        exp_sum = exp_sum + jnp.exp(rows_ref[k, 0:1, :] - top)
        total = total + rows_ref[k, 1:2, :]
    return top + jnp.log(exp_sum), total


def decoder_grads(counts, hidden, turned, rows, weights, place):
    wy, wd, zero, one, mixed, theta, sums, slopes = weights
    genes, cells = counts.shape
    padded = theta.shape[0]
    tile = gene_tile(padded)
    tiles = padded // tile
    half = CELL_BLOCK
    tc = 2 * half
    devices = rows.shape[0]

    def kernel(
        cnt_a, cnt_b, hid_ref, turned_ref, rows_ref, wy_ref, wd_ref, zero_ref, one_ref, mixed_ref,
        theta_ref, table_ref, slope_ref,
        x_ref, back_ref, mix_ref, sum_ref, scale_ref, drop_ref, col_ref, loss_ref,
        rhs, right, raw, scale_s, drop_s, acc, mix,
    ):
        @pl.when(pl.program_id(0) == 0)
        def _():
            scale_ref[...] = jnp.zeros(scale_ref.shape, F32)
            drop_ref[...] = jnp.zeros(drop_ref.shape, F32)
            col_ref[...] = jnp.zeros(col_ref.shape, F32)
            loss_ref[...] = jnp.zeros(loss_ref.shape, F32)

        lse, total = combine_rows(rows_ref)
        index = lax.broadcasted_iota(jnp.int32, (128, tc), 0)
        extra = jnp.where(index < 3, 1.0, 0.0)
        for k, row in enumerate(three_parts(jnp.log(total) - lse)):
            extra = jnp.where(index == k + 3, jnp.broadcast_to(row, (128, tc)), extra)
        rhs[0:128, :] = turned_ref[...]
        rhs[128:256, :] = extra.astype(BF16)
        right[:, 0:128] = hid_ref[...]
        lane = lax.broadcasted_iota(jnp.int32, (tc, 128), 1)
        right[:, 128:256] = jnp.where(lane == 0, 1.0, 0.0).astype(BF16)
        acc[...] = jnp.zeros(acc.shape, F32)
        mix[...] = jnp.zeros(mix.shape, F32)

        def rows_of(j):
            if isinstance(j, int):
                return pl.ds(j * tile, tile)
            return pl.ds(pl.multiple_of(j * tile, tile), tile)

        def products(j, slot):
            at = rows_of(j)
            raw[slot, 0:tile, :] = dot(wy_ref[at, :], rhs[...])
            raw[slot, tile : 2 * tile, :] = dot(wd_ref[at, :], rhs[...])

        def entries(j, slot, loss_acc, edge):
            base = j * tile
            for r in range(0, tile, 16):
                if isinstance(base, int):
                    at = pl.ds(base + r, 16)
                else:
                    at = pl.ds(pl.multiple_of(base + r, 16), 16)
                theta = theta_ref[at, :]
                theta = jnp.concatenate([theta, theta], 1)
                table = table_ref[at, :]
                slope_table = slope_ref[at, :]
                col = jnp.zeros((16, 128), F32)
                for side, cnt_ref in enumerate((cnt_a, cnt_b)):
                    span = slice(side * half, (side + 1) * half)
                    number = cnt_ref[at, :]
                    if edge and base + r + 16 > genes:
                        row = lax.broadcasted_iota(jnp.int32, number.shape, 0) + base + r
                        number = jnp.where(row < genes, number, 0)
                    y2 = raw[slot, r : r + 16, span] * LOG2E
                    d2 = raw[slot, tile + r : tile + r + 16, span] * LOG2E
                    held = jnp.minimum(d2, DROP_TOP)
                    x = jnp.exp2(y2)
                    x_one = 1.0 + x
                    lg = jnp.log2(x_one)
                    rc = pltpu.reciprocal(x_one, approx=True)
                    lift = theta * lg
                    keep = pltpu.reciprocal(1.0 + jnp.exp2(held), approx=True)
                    w_one = 1.0 + jnp.exp2(held + lift)
                    z = pltpu.reciprocal(w_one, approx=True)
                    none = number == 0
                    z = jnp.where(none, z, 1.0)
                    value = number.astype(F32)
                    zt = z * theta
                    x_ref[at, span] = x.astype(BF16)
                    scale_s[slot, r : r + 16, span] = (rc * (value + zt) - zt).astype(BF16)
                    drop_s[slot, r : r + 16, span] = (keep - z).astype(BF16)
                    like = jnp.log2(keep * jnp.where(none, w_one, 1.0)) - lift
                    like = like + value * (y2 - lg)
                    like = like + jnp.where(none, 0.0, held - d2)
                    loss_acc = loss_acc + (like[0:8] + like[8:16])
                    slope = z * lg
                    picked = []
                    for k in range(0, half, 128):
                        at_lane = number[:, k : k + 128]
                        picked.append(
                            jnp.take_along_axis(table, at_lane, axis=1, mode="promise_in_bounds")
                        )
                        col = col + (
                            jnp.take_along_axis(slope_table, at_lane, axis=1, mode="promise_in_bounds")
                            - slope[:, k : k + 128]
                        )
                    picked = jnp.concatenate(picked, 1)
                    loss_acc = loss_acc + (picked[0:8] + picked[8:16])
                col_ref[at, :] += col
            return loss_acc

        def gradients(j, slot):
            at = rows_of(j)
            scale_v = scale_s[slot]
            drop_v = drop_s[slot]
            acc[...] += dot(zero_ref[:, at], scale_v) + dot(one_ref[:, at], drop_v)
            mix[...] += dot(mixed_ref[:, at], x_ref[at, :])
            scale_ref[at, :] += dot(scale_v, right[...])
            drop_ref[at, :] += dot(drop_v, right[...])

        products(tiles - 1, 0)
        products(0, 1)
        loss_acc = entries(tiles - 1, 0, jnp.zeros((8, half), F32), True)

        def body(j, loss_acc):
            slot = lax.rem(j + 1, 2)
            products(jnp.minimum(j + 1, tiles - 2), 1 - slot)
            gradients(jnp.where(j == 0, tiles - 1, j - 1), 1 - slot)
            return entries(j, slot, loss_acc, False)

        loss_acc = lax.fori_loop(0, tiles - 1, body, loss_acc)
        gradients(tiles - 2, (tiles - 1) % 2)
        loss_ref[...] += loss_acc[:, 0:128] + loss_acc[:, 128:256]
        back_ref[...] = acc[0:128, :]
        for k in range(devices):
            sum_ref[k] = acc[128:129, :]
        mix_ref[...] = mix[...] * (1.0 / total)

    whole = lambda i: (0, 0)
    across = lambda i: (0, i)
    shape = jax.ShapeDtypeStruct
    return pl.pallas_call(
        kernel,
        grid=(cells // tc,),
        in_specs=[
            pl.BlockSpec((padded, half), lambda i: (0, place(2 * i))),
            pl.BlockSpec((padded, half), lambda i: (0, place(2 * i + 1))),
            pl.BlockSpec((tc, 128), lambda i: (i, 0)),
            pl.BlockSpec((128, tc), across),
            pl.BlockSpec((devices, 2, tc), lambda i: (0, 0, i)),
            pl.BlockSpec((padded, 256), whole),
            pl.BlockSpec((padded, 256), whole),
            pl.BlockSpec((144, padded), whole),
            pl.BlockSpec((144, padded), whole),
            pl.BlockSpec((128, padded), whole),
            pl.BlockSpec((padded, 128), whole),
            pl.BlockSpec((padded, 128), whole),
            pl.BlockSpec((padded, 128), whole),
        ],
        out_specs=[
            pl.BlockSpec((padded, tc), across),
            pl.BlockSpec((128, tc), across),
            pl.BlockSpec((128, tc), across),
            pl.BlockSpec((devices, 1, tc), lambda i: (0, 0, i)),
            pl.BlockSpec((padded, 256), whole),
            pl.BlockSpec((padded, 256), whole),
            pl.BlockSpec((padded, 128), whole),
            pl.BlockSpec((8, 128), whole),
        ],
        out_shape=[
            shape((padded, cells), BF16),
            shape((128, cells), F32),
            shape((128, cells), F32),
            shape((devices, 1, cells), F32),
            shape((padded, 256), F32),
            shape((padded, 256), F32),
            shape((padded, 128), F32),
            shape((8, 128), F32),
        ],
        scratch_shapes=[
            pltpu.VMEM((256, tc), BF16),
            pltpu.VMEM((tc, 256), BF16),
            pltpu.VMEM((2, 2 * tile, tc), F32),
            pltpu.VMEM((2, tile, tc), BF16),
            pltpu.VMEM((2, tile, tc), BF16),
            pltpu.VMEM((144, tc), F32),
            pltpu.VMEM((128, tc), F32),
        ],
        name="decoder_grads",
        **params(14 * cells * padded * 128, 6 * cells * padded),
    )(counts, counts, hidden, turned, rows, wy, wd, zero, one, mixed, theta, sums, slopes)


def decoder_weight_grads(x, turned, ratio_rows, scale, drop, col, theta, genes, total):
    padded, cells = x.shape
    tile = gene_tile(padded)

    def kernel(
        x_ref, turned_ref, ratio_ref, scale_ref, drop_ref, col_ref, theta_ref,
        out_ref, gene_ref, right, mingle,
    ):
        @pl.when(pl.program_id(0) == 0)
        def _():
            for k in range(cells // 128):
                span = slice(k * 128, (k + 1) * 128)
                ratio = ratio_ref[0:1, span]
                right[span, 0:128] = jnp.transpose(turned_ref[:, span].astype(F32) * ratio).astype(BF16)
                index = lax.broadcasted_iota(jnp.int32, (128, 128), 0)
                wide = jnp.where(index == 0, jnp.broadcast_to(ratio, (128, 128)), 0.0)
                right[span, 128:256] = jnp.transpose(wide).astype(BF16)

        theta = theta_ref[...]
        row = lax.broadcasted_iota(jnp.int32, (tile, 128), 0) + pl.program_id(0) * tile
        inside = row < genes
        less = dot(x_ref[...], right[...])
        both = scale_ref[...] - less * jnp.concatenate([theta, theta], 1)
        factor = -1.0 / total
        mingle[pl.ds(0, tile, stride=2), :] = jnp.where(inside, both[:, 0:128] * factor, 0.0)
        mingle[pl.ds(1, tile, stride=2), :] = jnp.where(inside, drop_ref[:, 0:128] * factor, 0.0)
        out_ref[...] = mingle[...].astype(BF16)
        lane = lax.broadcasted_iota(jnp.int32, (tile, 128), 1)
        first = lane == 0
        slope = (LN2 * theta) * col_ref[...] - jnp.where(first, scale_ref[:, 128:256], 0.0)
        rows = [
            jnp.transpose(both[:, 128:256])[0:1],
            jnp.transpose(drop_ref[:, 128:256])[0:1],
            jnp.sum(jnp.transpose(slope), axis=0, keepdims=True),
        ]
        wide = lax.broadcasted_iota(jnp.int32, (8, tile), 1) + pl.program_id(0) * tile
        gene_ref[...] = jnp.where(wide < genes, stack_rows(rows) * factor, 0.0)

    whole = lambda j: (0, 0)
    down = lambda j: (j, 0)
    return pl.pallas_call(
        kernel,
        grid=(padded // tile,),
        in_specs=[
            pl.BlockSpec((tile, cells), down),
            pl.BlockSpec((128, cells), whole),
            pl.BlockSpec((8, cells), whole),
            pl.BlockSpec((tile, 256), down),
            pl.BlockSpec((tile, 256), down),
            pl.BlockSpec((tile, 128), down),
            pl.BlockSpec((tile, 128), down),
        ],
        out_specs=[
            pl.BlockSpec((2 * tile, 128), down),
            pl.BlockSpec((8, tile), lambda j: (0, j)),
        ],
        out_shape=[
            jax.ShapeDtypeStruct((2 * padded, 128), BF16),
            jax.ShapeDtypeStruct((8, padded), F32),
        ],
        scratch_shapes=[pltpu.VMEM((cells, 256), BF16), pltpu.VMEM((2 * tile, 128), F32)],
        name="decoder_weight_grads",
        **params(2 * cells * padded * 128, 2 * cells * padded),
    )(x, turned, ratio_rows, scale, drop, col, theta)


def unit_slope(act, gate):
    return gate * (1.0 + act * (1.0 - gate))


def decoder_upstream(back, pre, sums, norm_param, total, lanes):
    average, inv = norm_rows(sums, None, total)
    normed = (pre - as_column(average, lanes)) * as_column(inv, lanes)
    act = normed * as_column(norm_param[2:3], lanes) + as_column(norm_param[3:4], lanes)
    return back.astype(F32) * unit_slope(act, sigmoid(act)), normed, inv


def decoder_back_stats(back, pre, sums, norm_param, total):
    cells = pre.shape[1]
    block = min(cells, LANE_BLOCK)

    def kernel(back_ref, pre_ref, s_ref, norm_ref, out_ref):
        up, normed, _ = decoder_upstream(
            back_ref[...], pre_ref[...], s_ref[...], norm_ref[...], total, block
        )
        rows = stack_rows([lane_sums_row(up), lane_sums_row(up * normed)])

        @pl.when(pl.program_id(0) == 0)
        def _():
            out_ref[...] = rows

        @pl.when(pl.program_id(0) > 0)
        def _():
            out_ref[...] += rows

    whole = lambda i: (0, 0)
    return pl.pallas_call(
        kernel,
        grid=(cells // block,),
        in_specs=[
            pl.BlockSpec((128, block), lambda i: (0, i)),
            pl.BlockSpec((128, block), lambda i: (0, i)),
            pl.BlockSpec((8, 128), whole),
            pl.BlockSpec((4, 128), whole),
        ],
        out_specs=pl.BlockSpec((8, 128), whole),
        out_shape=jax.ShapeDtypeStruct((8, 128), F32),
        name="decoder_back_stats",
        **params(30 * cells * 128, 6 * cells * 128),
    )(back, pre, sums, norm_param)


def middle_backward(back, pre, sums_two, back_sums, gathered, sums_one, norm_param, head_low, head_bias, dec_low, total):
    cells = pre.shape[1]
    block = min(cells, LANE_BLOCK)

    def kernel(
        back_ref, pre_ref, s2_ref, bs_ref, g_ref, s1_ref, norm_ref, head_ref, bias_ref, dec_ref,
        up_ref, out_ref, small_ref,
    ):
        up, normed, inv = decoder_upstream(
            back_ref[...], pre_ref[...], s2_ref[...], norm_ref[...], total, block
        )
        bs = bs_ref[...] * (1.0 / total)
        inner = up - as_column(bs[0:1], block) - normed * as_column(bs[1:2], block)
        pre_grad = inner * as_column(norm_ref[2:3] * inv, block)
        noise, label = unpack_extra(g_ref[128:160, :])
        normed_one, act, gate, enc_out, mean, log_var, spread, latent = head_terms(
            g_ref[0:128, :], s1_ref[...], norm_ref, head_ref, bias_ref, noise, total, block
        )
        dec_in = decoder_input(latent, label)
        high, low = two_parts(pre_grad)
        dec_grad = dot_nt(dec_in, high) + dot_nt(dec_in, low)
        dec_top = dec_ref[0:16, :]
        latent_grad = dot(dec_top, high) + dot(dec_top, low)
        mean_part = latent_grad + mean * (1.0 / total)
        var_part = latent_grad * noise * (0.5 * spread) + (jnp.exp(log_var) - 1.0) * (0.5 / total)
        parts = jnp.concatenate([mean_part, var_part], axis=0)
        parts_high, parts_low = two_parts(parts)
        head_grad = dot_nt(parts_high, enc_out) + dot_nt(parts_low, enc_out)
        out_grad = dot_tn(head_ref[...], parts_high) + dot_tn(head_ref[...], parts_low)
        up_one = out_grad * unit_slope(act, gate)
        up_ref[...] = up_one
        rows = stack_rows([lane_sums_row(up_one), lane_sums_row(up_one * normed_one)])
        bias_grad = parts[:, 0:128]
        for k in range(1, block // 128):
            bias_grad = bias_grad + parts[:, k * 128 : (k + 1) * 128]
        bias_grad = jnp.broadcast_to(jnp.sum(bias_grad, axis=1, keepdims=True), (32, 128))

        @pl.when(pl.program_id(0) == 0)
        def _():
            out_ref[...] = rows
            small_ref[0:144, :] = dec_grad
            small_ref[144:176, :] = head_grad
            small_ref[176:208, :] = bias_grad

        @pl.when(pl.program_id(0) > 0)
        def _():
            out_ref[...] += rows
            small_ref[0:144, :] += dec_grad
            small_ref[144:176, :] += head_grad
            small_ref[176:208, :] += bias_grad

    whole = lambda i: (0, 0)
    lanes = lambda i: (0, i)
    return pl.pallas_call(
        kernel,
        grid=(cells // block,),
        in_specs=[
            pl.BlockSpec((128, block), lanes),
            pl.BlockSpec((128, block), lanes),
            pl.BlockSpec((8, 128), whole),
            pl.BlockSpec((8, 128), whole),
            pl.BlockSpec((160, block), lanes),
            pl.BlockSpec((8, 128), whole),
            pl.BlockSpec((4, 128), whole),
            pl.BlockSpec((32, 128), whole),
            pl.BlockSpec((32, 128), whole),
            pl.BlockSpec((144, 128), whole),
        ],
        out_specs=[
            pl.BlockSpec((128, block), lanes),
            pl.BlockSpec((8, 128), whole),
            pl.BlockSpec((208, 128), whole),
        ],
        out_shape=[
            jax.ShapeDtypeStruct((128, cells), F32),
            jax.ShapeDtypeStruct((8, 128), F32),
            jax.ShapeDtypeStruct((208, 128), F32),
        ],
        name="middle_backward",
        **params(2 * cells * 128 * 800, 12 * cells * 128),
    )(back, pre, sums_two, back_sums, gathered, sums_one, norm_param, head_low, head_bias, dec_low)


def encoder_weight_grads(up, gathered, sums, back_sums, norm_param, counts, total, place):
    genes, cells = counts.shape
    padded = round_up(genes, 128)
    tile = gene_tile(padded)
    half = CELL_BLOCK
    tc = 2 * half

    def kernel(up_ref, g_ref, s_ref, bs_ref, norm_ref, cnt_a, cnt_b, out_ref, acc, xs):
        average, inv = norm_rows(s_ref[...], None, total)
        normed = (g_ref[...].astype(F32) - as_column(average, tc)) * as_column(inv, tc)
        bs = bs_ref[...] * (1.0 / total)
        inner = up_ref[...] - as_column(bs[0:1], tc) - normed * as_column(bs[1:2], tc)
        grad = jnp.transpose(inner * as_column(norm_ref[0:1] * inv, tc)).astype(BF16)

        @pl.when(pl.program_id(0) == 0)
        def _():
            acc[...] = jnp.zeros(acc.shape, F32)

        for j in range(padded // tile):
            for r in range(0, tile, 16):
                at = slice(j * tile + r, j * tile + r + 16)
                xs[at, 0:half] = log_counts(cnt_a[at, :], j * tile + r, genes)[1]
                xs[at, half:tc] = log_counts(cnt_b[at, :], j * tile + r, genes)[1]
            span = slice(j * tile, (j + 1) * tile)
            acc[span, :] += dot(xs[span, :], grad)

        @pl.when(pl.program_id(0) == pl.num_programs(0) - 1)
        def _():
            out_ref[...] = acc[...].astype(BF16)

    whole = lambda i: (0, 0)
    return pl.pallas_call(
        kernel,
        grid=(cells // tc,),
        in_specs=[
            pl.BlockSpec((128, tc), lambda i: (0, i)),
            pl.BlockSpec((128, tc), lambda i: (0, i)),
            pl.BlockSpec((8, 128), whole),
            pl.BlockSpec((8, 128), whole),
            pl.BlockSpec((4, 128), whole),
            pl.BlockSpec((padded, half), lambda i: (0, place(2 * i))),
            pl.BlockSpec((padded, half), lambda i: (0, place(2 * i + 1))),
        ],
        out_specs=pl.BlockSpec((padded, 128), whole),
        out_shape=jax.ShapeDtypeStruct((padded, 128), BF16),
        scratch_shapes=[pltpu.VMEM((padded, 128), F32), pltpu.VMEM((padded, tc), BF16)],
        name="encoder_weight_grads",
        **params(2 * cells * padded * 128, 4 * cells * padded),
    )(up, gathered, sums, back_sums, norm_param, counts, counts)


def adam_update(master, first, second, grad, rate):
    first_new = BETA_ONE * first + (1.0 - BETA_ONE) * grad
    second_new = BETA_TWO * second + (1.0 - BETA_TWO) * grad * grad
    first_hat = first_new * (1.0 / (1.0 - BETA_ONE**STEP))
    second_hat = second_new * (1.0 / (1.0 - BETA_TWO**STEP))
    master_new = master - rate * (
        first_hat / (jnp.sqrt(second_hat) + ADAM_EPS) + DECAY_RATE * master
    )
    return master_new, first_new, second_new


def adam_kernel(factor, enc_grad, out_grad, gene_grad, enc, out, gene):
    genes = enc[0].shape[0]
    padded = enc_grad.shape[0]
    tile = 2 * gene_tile(padded)

    def kernel(f_ref, eg_ref, og_ref, gg_ref, *refs):
        e_in, o_in, g_in = refs[0:3], refs[3:6], refs[6:9]
        e_out, o_out, g_out = refs[9:13], refs[13:17], refs[17:20]
        factor = f_ref[0:1, 0:1]
        for grad_ref, into, out_of, rate in (
            (eg_ref, e_in, e_out, G ** (-0.5)),
            (og_ref, o_in, o_out, H ** (-0.5)),
        ):
            for r in range(0, into[0].shape[0], 64):
                at = slice(r, r + 64)
                grad = grad_ref[at, :].astype(F32) * factor
                new = adam_update(into[0][at, :], into[1][at, :], into[2][at, :], grad, rate)
                for k in range(3):
                    out_of[k][at, :] = new[k]
                out_of[3][at, :] = new[0].astype(BF16)
        grad = gg_ref[0:3, :] * factor
        new = adam_update(g_in[0][...], g_in[1][...], g_in[2][...], grad, 0.3)
        for k in range(3):
            g_out[k][...] = new[k]

    e_spec = pl.BlockSpec((tile, 128), lambda j: (j, 0))
    o_spec = pl.BlockSpec((2 * tile, 128), lambda j: (j, 0))
    g_spec = pl.BlockSpec((3, tile), lambda j: (0, j))
    shape = jax.ShapeDtypeStruct
    return pl.pallas_call(
        kernel,
        grid=(-(-padded // tile),),
        in_specs=[
            pl.BlockSpec((8, 128), lambda j: (0, 0)),
            e_spec,
            o_spec,
            pl.BlockSpec((8, tile), lambda j: (0, j)),
        ]
        + [e_spec] * 3
        + [o_spec] * 3
        + [g_spec] * 3,
        out_specs=[e_spec] * 4 + [o_spec] * 4 + [g_spec] * 3,
        out_shape=[shape((genes, 128), F32)] * 3
        + [shape((genes, 128), BF16)]
        + [shape((2 * genes, 128), F32)] * 3
        + [shape((2 * genes, 128), BF16)]
        + [shape((3, genes), F32)] * 3,
        name="adam",
        **params(100 * 384 * padded, 28 * 384 * padded),
    )(factor, enc_grad, out_grad, gene_grad, *enc, *out, *gene)


def swap(value, axis, bit):
    return lax.ppermute(value, axis, [(k, k ^ bit) for k in range(lax.axis_size(axis))])


def steps_of(axis):
    bits = []
    bit = 1
    while bit < lax.axis_size(axis):
        bits.append(bit)
        bit *= 2
    return bits


def sum_all(value, axis):
    for bit in steps_of(axis):
        value = value + swap(value, axis, bit)
    return value


def my_bit(axis, bit):
    return (lax.axis_index(axis) // bit) % 2


def scatter_sum(value, axis, dim):
    for bit in steps_of(axis):
        half = value.shape[dim] // 2
        mine = my_bit(axis, bit)
        keep = lax.dynamic_slice_in_dim(value, mine * half, half, dim)
        send = lax.dynamic_slice_in_dim(value, (1 - mine) * half, half, dim)
        value = keep.astype(F32) + swap(send.astype(BF16), axis, bit).astype(F32)
    return value


def gather_parts(value, axis, dim):
    for bit in reversed(steps_of(axis)):
        other = swap(value, axis, bit)
        mine = my_bit(axis, bit)
        low = lax.select(mine == 0, value, other)
        high = lax.select(mine == 0, other, value)
        value = lax.concatenate([low, high], dim)
    return value


def spread_all(value, axis):
    devices = lax.axis_size(axis)
    copies = jnp.broadcast_to(value[None], (devices,) + value.shape)
    return lax.all_to_all(copies, axis, 0, 0, tiled=True)


def gene_rows(value):
    return value.transpose(2, 0, 1).reshape(-1, 128)


def from_gene_rows(value):
    return value.reshape(-1, 2, 128).transpose(1, 2, 0)


def squared(value):
    value = value.astype(F32)
    return jnp.sum(value * value)


def per_device(
    counts, labels, noise_draw, enc_weight, enc_first, enc_second, out_weight, out_first, out_second,
    gene_param, gene_first, gene_second, head_weight, head_first, head_second, head_bias, bias_first,
    bias_second, dec_weight, dec_first, dec_second, norm_param, norm_first, norm_second,
):
    gene_devs = lax.axis_size("gene")
    cell_devs = lax.axis_size("cell")
    cells, genes = counts.shape
    own = noise_draw.shape[0]
    total = cells * cell_devs
    padded = round_up(genes, 128)

    head_t = head_weight.T.astype(BF16)
    gap = jnp.zeros((6, 128), BF16)
    head_low = jnp.concatenate([head_t[:L], gap, head_t[L:], gap], 0)
    bias_gap = jnp.zeros((6,), F32)
    bias_col = jnp.concatenate([head_bias[:L], bias_gap, head_bias[L:], bias_gap])
    bias_col = jnp.broadcast_to(bias_col[:, None], (32, 128))
    dec_b = dec_weight.astype(BF16)
    dec_low = jnp.concatenate([dec_b[:L], gap, dec_b[L:]], 0)

    noise_t = noise_draw.T
    noise_high, noise_rest = two_parts(noise_t)
    label_row = labels.astype(BF16)[None]
    extra_gap = jnp.zeros((5, own), BF16)
    extra = jnp.concatenate(
        [noise_high, label_row, extra_gap, noise_rest, jnp.zeros((6, own), BF16)], 0
    )

    place = lambda i: turned_block(i, gene_devs, own // CELL_BLOCK)
    counts_t = counts.T
    partial, tot_rows = encoder_sums(counts_t, enc_weight, place)
    mine = scatter_sum(partial, "gene", 1)
    gathered = gather_parts(jnp.concatenate([mine.astype(BF16), extra], 0), "gene", 1)
    weights = decoder_weights(gene_rows(out_weight), gene_param)

    sums_one = sum_all(hidden_stats(gathered), "cell")
    pre, stats_two = encoder_heads(
        gathered, sums_one, norm_param, head_low, bias_col, dec_low, total
    )
    sums_two = sum_all(stats_two, "cell")
    hidden, turned, rows = decoder_scan(
        pre, sums_two, norm_param, tot_rows, weights[0], total, gene_devs
    )
    rows = lax.all_to_all(rows, "gene", 0, 0, tiled=True)
    x_soft, back_part, mix, scale_sum, scale, drop, col, loss_rows = decoder_grads(
        counts_t, hidden, turned, rows, weights, place
    )
    cell_sum = jnp.sum(lax.all_to_all(scale_sum, "gene", 0, 0, tiled=True), 0)
    cell_total = jnp.sum(rows[:, 1], 0)[None]
    back_part = (back_part - cell_sum * mix) * (-1.0 / total)
    ratio = jnp.broadcast_to(cell_sum / cell_total, (8, cells))
    out_grad, gene_grad = decoder_weight_grads(
        x_soft, turned, ratio, scale, drop, col, weights[5], genes, total
    )
    back = gather_parts(scatter_sum(back_part, "gene", 1).astype(BF16), "gene", 1)
    back_stats = sum_all(decoder_back_stats(back, pre, sums_two, norm_param, total), "cell")
    up_one, enc_stats, small = middle_backward(
        back, pre, sums_two, back_stats, gathered, sums_one, norm_param, head_low, bias_col, dec_low,
        total,
    )
    enc_back = sum_all(enc_stats, "cell")
    enc_grad = encoder_weight_grads(
        up_one, gathered, sums_one, enc_back, norm_param, counts_t, total, place
    )

    out_mine = scatter_sum(out_grad, "cell", 0)
    enc_mine = scatter_sum(enc_grad, "cell", 0)
    gene_grad = sum_all(gene_grad, "cell")
    small = sum_all(small, "cell")
    out_all = gather_parts(out_mine.astype(BF16), "cell", 0)
    enc_all = gather_parts(enc_mine.astype(BF16), "cell", 0)

    dec_grad = jnp.concatenate([small[:L], small[16:144]], 0)
    head_grad = jnp.concatenate([small[144 : 144 + L], small[160 : 160 + L]], 0).T
    bias_grad = jnp.concatenate([small[176 : 176 + L, 0], small[192 : 192 + L, 0]])
    norm_grad = jnp.stack([enc_back[1], enc_back[0], back_stats[1], back_stats[0]])
    squares = (
        squared(enc_mine) + squared(out_mine) + squared(gene_grad) * (1.0 / cell_devs)
    )
    recon = -LN2 * jnp.sum(loss_rows)
    pair = jnp.broadcast_to(jnp.stack([squares, recon])[:, None], (2, 128))
    pair = jnp.sum(spread_all(pair, ("gene", "cell")), 0)
    loss_sum = pair[1, 0] + jnp.sum(sums_two[2])
    grad_norm = jnp.sqrt(
        pair[0, 0] + squared(head_grad) + squared(bias_grad) + squared(dec_grad) + squared(norm_grad)
    )
    factor = jnp.minimum(1.0, CLIP_NORM / (grad_norm + 1e-06))
    new = adam_kernel(
        jnp.broadcast_to(factor, (8, 128)),
        enc_all,
        out_all,
        gene_grad,
        (enc_weight, enc_first, enc_second),
        (gene_rows(out_weight), gene_rows(out_first), gene_rows(out_second)),
        (gene_param, gene_first, gene_second),
    )
    enc_new, gene_new = new[0:4], new[8:11]
    out_new = [from_gene_rows(value) for value in new[4:8]]
    head_new = adam_update(head_weight, head_first, head_second, head_grad * factor, H ** (-0.5))
    bias_new = adam_update(head_bias, bias_first, bias_second, bias_grad * factor, 0.3)
    dec_new = adam_update(dec_weight, dec_first, dec_second, dec_grad * factor, (L + NB) ** (-0.5))
    norm_new = adam_update(norm_param, norm_first, norm_second, norm_grad * factor, 0.3)
    return (
        loss_sum,
        grad_norm,
        *enc_new[0:3],
        *out_new[0:3],
        *gene_new,
        *head_new,
        *bias_new,
        *dec_new,
        *norm_new,
        enc_new[3],
        out_new[3],
        head_new[0].astype(BF16),
        dec_new[0].astype(BF16),
    )


def solution(mesh):
    rows = P("gene", None)
    columns = P(None, None, "gene")
    genes = P(None, "gene")
    in_specs = (P("cell", "gene"), P(("cell", "gene")), P(("cell", "gene"), None))
    in_specs += (rows,) * 3 + (columns,) * 3 + (genes,) * 3 + (P(),) * 12
    out_specs = (P(), P()) + (rows,) * 3 + (columns,) * 3 + (genes,) * 3 + (P(),) * 12
    out_specs += (rows, columns, P(), P())
    return jax.shard_map(
        per_device, mesh=mesh, in_specs=in_specs, out_specs=out_specs, check_vma=False
    )
```
